1024 devices in a mesh: dp: 4 (over y_lo, core), blk: 32 (over y_hi, z), hid: 8 (over x).
Axes of the slice: x: 8, y: 8 (y_hi: 4, y_lo: 2; y = y_hi * 2 + y_lo), z: 8, core: 2. Of those that a mesh axis runs over, the one named last changes fastest.
Arguments:
- tokens: bfloat16 [1024, 4096], P('dp', 'blk'), may hold values from -6 to 6
- cotangent: bfloat16 [1024, 4096], P('dp', 'blk'), may hold values from -2 to 2
- gate_weight: bfloat16 [14336, 4096], P('hid', 'blk'), may hold values from -0.09375 to 0.09375
- up_weight: bfloat16 [14336, 4096], P('hid', 'blk'), may hold values from -0.09375 to 0.09375
- down_weight: bfloat16 [14336, 4096], P('hid', 'blk'), may hold values from -0.046875 to 0.046875
Outputs:
- input_grad: float32 [1024, 4096], P(('dp', 'hid'), 'blk')
- gate_grad: float32 [14336, 4096], P('hid', ('blk', 'dp'))
- up_grad: float32 [14336, 4096], P('hid', ('blk', 'dp'))
- down_grad: float32 [14336, 4096], P('hid', ('blk', 'dp'))
The draws below stay inside these ranges and needn't reach their ends.
All inputs are finite; a program needn't handle non-finite values.
Results may differ from the reference program's by a relative error of at most 0.0029.
Values may be sent and summed in bfloat16 or wider, within the bound.
A program may use at most 32 MiB of HBM per device.

```python
import jax
import jax.numpy as jnp
from jax import lax

D = 4096
FF = 14336
TOK_DEV = 8
TOKENS = 1024
N_DP = 4
N_BLK = 32


def raised(entries, key, source, target, parts, factor):
    owner, partner = [(jnp.arange(entries.shape[axis_at]) // (entries.shape[axis_at] // parts)).reshape([-1 if axis == axis_at else 1 for axis in range(entries.ndim)]) for axis_at in (source, target)]
    chosen = jax.random.permutation(key, parts)[partner]
    strong = (owner == chosen) | (owner == (partner + parts // 2) % parts)
    return jnp.where(strong, factor * entries, entries)


def level_of(rng, dims, pieces, least, top_value):
    gain, own = 1.0, jax.random.fold_in(rng, 6)
    for position, blocks in pieces:
        steps = jnp.exp(jax.random.uniform(jax.random.fold_in(own, position), (blocks,), jnp.float32, least / len(pieces), top_value / len(pieces)))
        gain = gain * jnp.repeat(steps, dims[position] // blocks).reshape([-1 if axis == position else 1 for axis in range(len(dims))])
    return gain


def bell_draw(rng, shape, spread, reach, pieces=(), kind=jnp.bfloat16):
    result = spread * jax.random.normal(rng, shape, jnp.float32)
    if pieces:
        result = result * level_of(rng, shape, pieces, -0.22, 0.18)
    return jnp.clip(result, -reach, reach).astype(kind)


def heavy_noise(rng, extent, width, limit, split, heavy, held_as=jnp.bfloat16):
    array = width * jax.random.normal(rng, extent, jnp.float32)
    if split:
        array = array * level_of(rng, extent, split, -0.22, 0.18)
    return jnp.clip(raised(array, jax.random.fold_in(rng, 3), *heavy), -limit, limit).astype(held_as)


def setup_inputs(seed: int = 0) -> dict:
    key_list = jax.random.split(jax.random.key(seed), 6)
    tokens = heavy_noise(key_list[0], (TOKENS, D), 1.0, 6.0, ((0, 4), (1, 32)), (1, 0, 32, 2.75))
    cotangent = heavy_noise(key_list[1], (TOKENS, D), 0.3, 2.0, ((0, 4), (1, 32)), (1, 0, 32, 2.75))
    gate_weight = bell_draw(key_list[2], (FF, D), D ** -0.5, 0.09375, ((0, 8), (1, 32)))
    up_weight = bell_draw(key_list[3], (FF, D), D ** -0.5, 0.09375, ((0, 8), (1, 32)))
    down_weight = bell_draw(key_list[4], (FF, D), FF ** -0.5, 0.046875, ((0, 8), (1, 32)))
    return dict(tokens=tokens, cotangent=cotangent, gate_weight=gate_weight, up_weight=up_weight, down_weight=down_weight)


contract_last = (((1,), (1,)), ((), ()))
contract_first = (((0,), (0,)), ((), ()))


def replica(token_block, cotan_block, gate_weight, up_weight, down_weight):
    gate_pre = lax.dot_general(token_block, gate_weight, contract_last, preferred_element_type=jnp.float32)
    up_pre = lax.dot_general(token_block, up_weight, contract_last, preferred_element_type=jnp.float32)
    grad_hidden = lax.dot_general(cotan_block, down_weight, contract_last, preferred_element_type=jnp.float32)
    sigmoid_gate = jax.nn.sigmoid(gate_pre)
    silu_gate = gate_pre * sigmoid_gate
    hidden = (silu_gate * up_pre).astype(jnp.bfloat16)
    grad_up = (grad_hidden * silu_gate).astype(jnp.bfloat16)
    grad_gate = (grad_hidden * up_pre * sigmoid_gate * (1.0 + gate_pre * (1.0 - sigmoid_gate))).astype(jnp.bfloat16)
    input_grad = jnp.dot(grad_gate, gate_weight, preferred_element_type=jnp.float32)
    input_grad = input_grad + jnp.dot(grad_up, up_weight, preferred_element_type=jnp.float32)
    gate_part = lax.dot_general(grad_gate, token_block, contract_first, preferred_element_type=jnp.float32)
    up_part = lax.dot_general(grad_up, token_block, contract_first, preferred_element_type=jnp.float32)
    down_part = lax.dot_general(hidden, cotan_block, contract_first, preferred_element_type=jnp.float32)
    return input_grad, gate_part, up_part, down_part


def reference(tokens, cotangent, gate_weight, up_weight, down_weight):
    replica_rows = TOK_DEV * N_BLK
    grads_in = []
    gate_grad = jnp.zeros(gate_weight.shape, jnp.float32)
    up_grad = jnp.zeros(gate_weight.shape, jnp.float32)
    down_grad = jnp.zeros(gate_weight.shape, jnp.float32)
    for index in range(N_DP):
        token_block = tokens[index * replica_rows:(index + 1) * replica_rows]
        cotan_block = cotangent[index * replica_rows:(index + 1) * replica_rows]
        input_part, gate_part, up_part, down_part = replica(token_block, cotan_block, gate_weight, up_weight, down_weight)
        grads_in.append(input_part)
        gate_grad = gate_grad + gate_part
        up_grad = up_grad + up_part
        down_grad = down_grad + down_part
    return jnp.concatenate(grads_in, axis=0), gate_grad, up_grad, down_grad
```

```python
import jax
import jax.numpy as jnp
from jax import lax
from jax.experimental import pallas as pl
from jax.experimental.pallas import tpu as pltpu
from jax.sharding import PartitionSpec as P

MESH = pl.DeviceIdType.MESH
NZ, NY, NX = 8, 4, 8
LANES = 128
CHUNKS = (128, 96)
F32, BF16 = jnp.float32, jnp.bfloat16
contract_last = (((1,), (1,)), ((), ()))
contract_first = (((0,), (0,)), ((), ()))
FAR_FIRST = (4, 3, 5, 2, 6, 1, 7)


def kernel(
    tok_in, cot_in, gate_w, up_w, down_w,
    ig_out, gate_out, up_out, down_out,
    tok, ig_send, ig_recv, ig_sum, ig_blocks,
    *rest,
):
    n_chunks = len(CHUNKS)
    names = ("g", "p", "rp", "h", "wg", "cr", "ls", "lr", "fs", "fr")
    bufs = []
    for k in range(n_chunks):
        bufs.append(dict(zip(names, rest[k * len(names):(k + 1) * len(names)])))
    (
        tz_s, tz_r, xr_s, xr_r, own_s,
        a_s, a_r, f_s, f_r, r_s, r_r, y_s, y_r, c_s, c_r, l_s, l_r, z_s, z_r,
        ix_s, ix_r, iz_s, iz_r,
    ) = rest[n_chunks * len(names):]

    dp = lax.axis_index("dp")
    blk = lax.axis_index("blk")
    x = lax.axis_index("hid")
    yh, z = blk // NZ, blk % NZ
    yl, c = dp // 2, dp % 2
    units = gate_w.shape[0] // NZ
    offs = [sum(CHUNKS[:k]) for k in range(n_chunks)]

    def at_z(v):
        return (dp, yh * NZ + v, x)

    def at_y(v):
        return (dp, v * NZ + z, x)

    def at_x(v):
        return (dp, blk, v)

    sibling = (yl * 2 + 1 - c, blk, x)
    across = ((1 - yl) * 2 + c, blk, x)

    def zj(j):
        return lax.rem(z + j, NZ)

    def yj(j):
        return lax.rem(yh + j, NY)

    def xj(j):
        return lax.rem(x + j, NX)

    barrier = pltpu.get_barrier_semaphore()
    peers = [at_z(zj(j)) for j in range(1, NZ)]
    peers += [at_x(xj(j)) for j in range(1, NX)]
    peers += [at_y(yj(j)) for j in range(1, NY)]
    peers += [sibling, across]
    for p in peers:
        pl.semaphore_signal(barrier, inc=1, device_id=p, device_id_type=MESH)
    pl.semaphore_wait(barrier, len(peers))

    pending = []

    def remote(src, dst, ss, rs, dev):
        return pltpu.make_async_remote_copy(
            src_ref=src, dst_ref=dst, send_sem=ss, recv_sem=rs,
            device_id=dev, device_id_type=MESH,
        )

    def go(copies):
        for cp in copies:
            cp.start()
        pending.extend(copies)
        return copies

    def arrived(copies):
        for cp in copies:
            cp.wait_recv()

    rows_x = tok_in.shape[0] // NX
    my_rows = pl.ds(pl.multiple_of(x * rows_x, rows_x), rows_x)
    my_lanes = pl.ds(pl.multiple_of(z * LANES, LANES), LANES)
    ins = (tok_in, cot_in)
    tz = go([
        remote(ins[a].at[my_rows, :], tok.at[a, my_rows, my_lanes], tz_s.at[a, j], tz_r.at[a, j], at_z(zj(j)))
        for j in FAR_FIRST for a in range(2)
    ])
    weights = (gate_w, up_w, down_w)

    def w_rows(k, to):
        nh = CHUNKS[k] // 2
        return pl.ds(pl.multiple_of(to * units + offs[k] + c * nh, 16), nh)

    def half(k, who):
        nh = CHUNKS[k] // 2
        return pl.ds(pl.multiple_of(who * nh, 16), nh)

    def push_weights(k):
        g = bufs[k]["g"]
        return go([
            remote(weights[m].at[w_rows(k, zj(j)), :], g.at[m, half(k, c), my_lanes], a_s.at[k, m, j], a_r.at[k, m, j], at_z(zj(j)))
            for j in FAR_FIRST for m in range(3)
        ])

    owns = []
    a_copies = [push_weights(0)]
    for a in range(2):
        owns.append(pltpu.make_async_copy(ins[a].at[my_rows, :], tok.at[a, my_rows, my_lanes], own_s.at[a]))
    for k in range(n_chunks):
        for m in range(3):
            owns.append(pltpu.make_async_copy(
                weights[m].at[w_rows(k, z), :], bufs[k]["g"].at[m, half(k, c), my_lanes], own_s.at[2 + k * 3 + m]))
    for cp in owns:
        cp.start()
    for k in range(1, n_chunks):
        a_copies.append(push_weights(k))
    for cp in owns:
        cp.wait()
    arrived(tz)

    def slice_at(d):
        return pl.ds(pl.multiple_of(lax.rem(x + d + NX, NX) * rows_x, rows_x), rows_x)

    for t in range(1, NX // 2 + 1):
        if t < NX // 2:
            right_ref, left_ref = tok.at[:, slice_at(1 - t), :], tok.at[:, slice_at(t - 1), :]
        else:
            right_ref, left_ref = tok.at[0, slice_at(1 - t), :], tok.at[1, slice_at(t - 1), :]
        step = go([
            remote(right_ref, right_ref, xr_s.at[0, t - 1], xr_r.at[0, t - 1], at_x(xj(1))),
            remote(left_ref, left_ref, xr_s.at[1, t - 1], xr_r.at[1, t - 1], at_x(xj(NX - 1))),
        ])
        if t == 1:
            arrived(a_copies[0])
            g0 = bufs[0]["g"].at[:, half(0, c), :]
            f_copies = [go([remote(g0, g0, f_s.at[0], f_r.at[0], sibling)])]
        arrived(step)

    def forward(k):
        arrived(a_copies[k])
        g = bufs[k]["g"].at[:, half(k, c), :]
        f_copies.append(go([remote(g, g, f_s.at[k], f_r.at[k], sibling)]))

    rows_y = tok_in.shape[0] // NY

    def project(k):
        arrived(f_copies[k])
        b = bufs[k]
        for m in range(3):
            part = lax.dot_general(tok[m // 2], b["g"][m], contract_last, preferred_element_type=F32)
            for q in range(NY):
                b["p"][q, m] = part[q * rows_y:(q + 1) * rows_y]
        return go([
            remote(b["p"].at[yj(j)], b["rp"].at[j - 1], r_s.at[k, j], r_r.at[k, j], at_y(yj(j)))
            for j in (2, 1, 3)
        ])

    def activate(k, copies):
        arrived(copies)
        b = bufs[k]
        gate_pre, up_pre, grad_hidden = [
            b["p"][yh, m] + b["rp"][0, m] + b["rp"][1, m] + b["rp"][2, m] for m in range(3)
        ]
        s = jax.nn.sigmoid(gate_pre)
        silu = gate_pre * s
        b["h"][yh, 0] = (grad_hidden * up_pre * s * (1.0 + gate_pre * (1.0 - s))).astype(BF16)
        b["h"][yh, 1] = (grad_hidden * silu).astype(BF16)
        b["h"][yh, 2] = (silu * up_pre).astype(BF16)
        mine = b["h"].at[yh]
        return go([
            remote(mine, mine, y_s.at[k, j], y_r.at[k, j], at_y(yj(j))) for j in (2, 1, 3)
        ])

    def backward(k, copies):
        arrived(copies)
        b = bufs[k]
        n = CHUNKS[k]
        grads = [
            jnp.concatenate([b["h"][q, m] for q in range(NY)], axis=0) for m in range(3)
        ]
        for m in range(3):
            full = lax.dot_general(tok[m // 2], grads[m], contract_first, preferred_element_type=F32)
            b["wg"][m] = full.reshape(NZ, 2, 2, LANES // 4, n)
        copies = go([remote(b["wg"].at[:, :, :, 1 - c], b["cr"], c_s.at[k], c_r.at[k], sibling)])
        part = jnp.dot(grads[0], b["g"][0], preferred_element_type=F32)
        part = part + jnp.dot(grads[1], b["g"][1], preferred_element_type=F32)
        return copies, part

    def over_y(k, copies):
        arrived(copies)
        b = bufs[k]
        b["ls"][...] = (b["wg"][:, :, 1 - yl, c] + b["cr"][:, :, 1 - yl]).astype(BF16)
        return go([remote(b["ls"], b["lr"], l_s.at[k], l_r.at[k], across)])

    def over_z(k, copies):
        arrived(copies)
        b = bufs[k]
        for m in range(3):
            done = b["wg"][m, :, yl, c] + b["cr"][m, :, yl] + b["lr"][m].astype(F32)
            b["fs"][:, m] = done.astype(BF16)
        b["fr"][z] = b["fs"][z]
        return go([
            remote(b["fs"].at[zj(j)], b["fr"].at[z], z_s.at[k, j], z_r.at[k, j], at_z(zj(j)))
            for j in FAR_FIRST
        ])

    outs = (gate_out, up_out, down_out)

    def finish(k, copies):
        arrived(copies)
        b = bufs[k]
        for q in range(NZ):
            for m in range(3):
                outs[m][q * units + offs[k]:q * units + offs[k] + CHUNKS[k], :] = b["fr"][q, m].astype(F32).T

    r0 = project(0)
    forward(1)
    y0 = activate(0, r0)
    r1 = project(1)
    c0, ig0 = backward(0, y0)
    ig_sum[...] = ig0
    y1 = activate(1, r1)
    l0 = over_y(0, c0)
    c1, ig1 = backward(1, y1)
    total = ig_sum[...] + ig1
    ig_sum[...] = total
    for q in range(NX):
        ig_send[q] = total[q * rows_x:(q + 1) * rows_x].astype(BF16)
    ix = go([
        remote(ig_send.at[xj(j)], ig_recv.at[j], ix_s.at[j], ix_r.at[j], at_x(xj(j))) for j in FAR_FIRST
    ])
    z0 = over_z(0, l0)
    l1 = over_y(1, c1)
    finish(0, z0)
    z1 = over_z(1, l1)
    arrived(ix)
    mine = ig_sum[my_rows, :]
    for j in range(1, NX):
        mine = mine + ig_recv[j].astype(F32)
    for q in range(NZ):
        ig_blocks[0, q] = mine[:, q * LANES:(q + 1) * LANES]
    iz = go([
        remote(ig_blocks.at[0, zj(j)], ig_blocks.at[1, j], iz_s.at[j], iz_r.at[j], at_z(zj(j))) for j in FAR_FIRST
    ])
    finish(1, z1)
    arrived(iz)
    result = ig_blocks[0, z]
    for j in range(1, NZ):
        result = result + ig_blocks[1, j]
    ig_out[...] = result
    for cp in pending:
        cp.wait_send()


def local(tokens, cotangent, gate_weight, up_weight, down_weight):
    rows, units_all = tokens.shape[0], gate_weight.shape[0]
    wide = NZ * LANES
    feats = LANES // 4
    scratch = [
        pltpu.VMEM((2, rows, wide), BF16),
        pltpu.VMEM((NX, rows // NX, wide), BF16),
        pltpu.VMEM((NX, rows // NX, wide), BF16),
        pltpu.VMEM((rows, wide), F32),
        pltpu.VMEM((2, NZ, rows // NX, LANES), F32),
    ]
    for n in CHUNKS:
        scratch += [
            pltpu.VMEM((3, n, wide), BF16),
            pltpu.VMEM((NY, 3, rows // NY, n), F32),
            pltpu.VMEM((NY - 1, 3, rows // NY, n), F32),
            pltpu.VMEM((NY, 3, rows // NY, n), BF16),
            pltpu.VMEM((3, NZ, 2, 2, feats, n), F32),
            pltpu.VMEM((3, NZ, 2, feats, n), F32),
            pltpu.VMEM((3, NZ, feats, n), BF16),
            pltpu.VMEM((3, NZ, feats, n), BF16),
            pltpu.VMEM((NZ, 3, feats, n), BF16),
            pltpu.VMEM((NZ, 3, feats, n), BF16),
        ]
    nc = len(CHUNKS)
    dma = pltpu.SemaphoreType.DMA
    scratch += [dma((2, NZ)), dma((2, NZ)), dma((2, NX // 2)), dma((2, NX // 2)), dma((2 + 3 * nc,))]
    for shape in ((nc, 3, NZ), (nc,), (nc, NY), (nc, NY), (nc,), (nc,), (nc, NZ), (NX,), (NZ,)):
        scratch += [dma(shape), dma(shape)]
    vmem = pl.BlockSpec(memory_space=pltpu.VMEM)
    grad = jax.ShapeDtypeStruct((units_all, feats), F32)
    return pl.pallas_call(
        kernel,
        out_shape=(jax.ShapeDtypeStruct((rows // NX, LANES), F32), grad, grad, grad),
        in_specs=[pl.BlockSpec(memory_space=pl.ANY)] * 5,
        out_specs=(vmem,) * 4,
        scratch_shapes=scratch,
        compiler_params=pltpu.CompilerParams(
            collective_id=0, has_side_effects=True, vmem_limit_bytes=48 * 2**20
        ),
    )(tokens, cotangent, gate_weight, up_weight, down_weight)


def solution(mesh):
    return jax.shard_map(
        local,
        mesh=mesh,
        in_specs=(
            P("dp", "blk"),
            P("dp", "blk"),
            P("hid", "blk"),
            P("hid", "blk"),
            P("hid", "blk"),
        ),
        out_specs=(
            P(("dp", "hid"), "blk"),
            P("hid", ("blk", "dp")),
            P("hid", ("blk", "dp")),
            P("hid", ("blk", "dp")),
        ),
        check_vma=False,
    )
```

```python
import jax
import jax.numpy as jnp
from jax import lax
from jax.experimental import pallas as pl
from jax.experimental.pallas import tpu as pltpu
from jax.sharding import PartitionSpec as P

MESH = pl.DeviceIdType.MESH
NZ, NY, NX = 8, 4, 8
LANES = 128
CHUNKS = (128, 96)
F32, BF16 = jnp.float32, jnp.bfloat16
contract_last = (((1,), (1,)), ((), ()))
contract_first = (((0,), (0,)), ((), ()))
FAR_FIRST = (4, 3, 5, 2, 6, 1, 7)


def kernel(
    tok_in, cot_in, gate_w, up_w, down_w,
    ig_out, grad_out,
    tok_own, w_own, tok, ig_send, ig_recv, ig_sum, ig_blocks,
    *rest,
):
    n_chunks = len(CHUNKS)
    names = ("g", "p", "rp", "h", "wg", "cr", "ls", "lr", "fs", "fr")
    bufs = []
    for k in range(n_chunks):
        bufs.append(dict(zip(names, rest[k * len(names):(k + 1) * len(names)])))
    (
        in_s, tz_s, tz_r, xr_s, xr_r, own_s,
        a_s, a_r, f_s, f_r, r_s, r_r, y_s, y_r, c_s, c_r, l_s, l_r, z_s, z_r,
        ix_s, ix_r, iz_s, iz_r,
    ) = rest[n_chunks * len(names):]

    dp = lax.axis_index("dp")
    blk = lax.axis_index("blk")
    x = lax.axis_index("hid")
    yh, z = blk // NZ, blk % NZ
    yl, c = dp // 2, dp % 2
    bases = [NZ * sum(CHUNKS[:k]) for k in range(n_chunks)]

    loads = []
    for i, ref in enumerate((tok_in, cot_in)):
        loads.append(pltpu.make_async_copy(ref, tok_own.at[i], in_s.at[i]))
    for i, ref in enumerate((gate_w, up_w, down_w)):
        loads.append(pltpu.make_async_copy(ref, w_own.at[i], in_s.at[2 + i]))
    for cp in loads:
        cp.start()

    def at_z(v):
        return (dp, yh * NZ + v, x)

    def at_y(v):
        return (dp, v * NZ + z, x)

    def at_x(v):
        return (dp, blk, v)

    sibling = (yl * 2 + 1 - c, blk, x)
    across = ((1 - yl) * 2 + c, blk, x)

    def zj(j):
        return lax.rem(z + j, NZ)

    def yj(j):
        return lax.rem(yh + j, NY)

    def xj(j):
        return lax.rem(x + j, NX)

    barrier = pltpu.get_barrier_semaphore()
    peers = [at_z(zj(j)) for j in range(1, NZ)]
    peers += [at_x(xj(j)) for j in range(1, NX)]
    peers += [at_y(yj(j)) for j in range(1, NY)]
    peers += [sibling, across]
    for p in peers:
        pl.semaphore_signal(barrier, inc=1, device_id=p, device_id_type=MESH)
    pl.semaphore_wait(barrier, len(peers))

    pending = []

    def remote(src, dst, ss, rs, dev):
        return pltpu.make_async_remote_copy(
            src_ref=src, dst_ref=dst, send_sem=ss, recv_sem=rs,
            device_id=dev, device_id_type=MESH,
        )

    def go(copies):
        for cp in copies:
            cp.start()
        pending.extend(copies)
        return copies

    def arrived(copies):
        for cp in copies:
            cp.wait_recv()

    rows_x = tok_in.shape[0] // NX
    my_rows = pl.ds(pl.multiple_of(x * rows_x, rows_x), rows_x)
    my_lanes = pl.ds(pl.multiple_of(z * LANES, LANES), LANES)
    loads[0].wait()
    loads[1].wait()
    tz = go([
        remote(tok_own.at[:, my_rows, :], tok.at[:, my_rows, my_lanes], tz_s.at[j], tz_r.at[j], at_z(zj(j)))
        for j in FAR_FIRST
    ])

    def w_rows(k, to):
        nh = CHUNKS[k] // 2
        return pl.ds(pl.multiple_of(bases[k] + to * CHUNKS[k] + c * nh, 16), nh)

    def half(k, who):
        nh = CHUNKS[k] // 2
        return pl.ds(pl.multiple_of(who * nh, 16), nh)

    def push_weights(k):
        g = bufs[k]["g"]
        return go([
            remote(w_own.at[:, w_rows(k, zj(j)), :], g.at[:, half(k, c), my_lanes], a_s.at[k, j], a_r.at[k, j], at_z(zj(j)))
            for j in FAR_FIRST
        ])

    for cp in loads[2:]:
        cp.wait()
    a_copies = [push_weights(0)]
    owns = [pltpu.make_async_copy(tok_own.at[:, my_rows, :], tok.at[:, my_rows, my_lanes], own_s.at[0])]
    for k in range(n_chunks):
        owns.append(pltpu.make_async_copy(
            w_own.at[:, w_rows(k, z), :], bufs[k]["g"].at[:, half(k, c), my_lanes], own_s.at[1 + k]))
    for cp in owns:
        cp.start()
    for cp in owns:
        cp.wait()
    arrived(tz)

    f_copies = []

    def forward(k):
        arrived(a_copies[k])
        g = bufs[k]["g"].at[:, half(k, c), :]
        f_copies.append(go([remote(g, g, f_s.at[k], f_r.at[k], sibling)]))

    part = rows_x // 2

    def slice_at(d, i):
        row = lax.rem(x + d + NX, NX) * rows_x + i % 2 * part
        return i // 2, pl.ds(pl.multiple_of(row, part), part)

    moving = {}
    for t in range(1, NX // 2 + 1):
        for i in range(4):
            for way in range(2):
                if t > 1:
                    arrived(moving.pop((t - 1, i, way)))
            for way in range(2):
                if t == NX // 2 and i // 2 != way:
                    continue
                a, where = slice_at(1 - t if way == 0 else t - 1, i)
                ref = tok.at[a, where, :]
                moving[t, i, way] = go([
                    remote(ref, ref, xr_s.at[way, t - 1, i], xr_r.at[way, t - 1, i], at_x(xj(1 if way == 0 else NX - 1)))
                ])
        if t == 3:
            forward(0)
            a_copies.append(push_weights(1))
    for copies in moving.values():
        arrived(copies)

    rows_y = tok_in.shape[0] // NY

    def project(k):
        arrived(f_copies[k])
        b = bufs[k]
        for m in range(3):
            part = lax.dot_general(tok[m // 2], b["g"][m], contract_last, preferred_element_type=F32)
            for q in range(NY):
                b["p"][q, m] = part[q * rows_y:(q + 1) * rows_y]
        return go([
            remote(b["p"].at[yj(j)], b["rp"].at[j - 1], r_s.at[k, j], r_r.at[k, j], at_y(yj(j)))
            for j in (2, 1, 3)
        ])

    def activate(k, copies):
        arrived(copies)
        b = bufs[k]
        gate_pre, up_pre, grad_hidden = [
            b["p"][yh, m] + b["rp"][0, m] + b["rp"][1, m] + b["rp"][2, m] for m in range(3)
        ]
        s = jax.nn.sigmoid(gate_pre)
        silu = gate_pre * s
        b["h"][yh, 0] = (grad_hidden * up_pre * s * (1.0 + gate_pre * (1.0 - s))).astype(BF16)
        b["h"][yh, 1] = (grad_hidden * silu).astype(BF16)
        b["h"][yh, 2] = (silu * up_pre).astype(BF16)
        mine = b["h"].at[yh]
        return go([
            remote(mine, mine, y_s.at[k, j], y_r.at[k, j], at_y(yj(j))) for j in (2, 1, 3)
        ])

    def backward(k, copies):
        arrived(copies)
        b = bufs[k]
        n = CHUNKS[k]
        grads = [
            jnp.concatenate([b["h"][q, m] for q in range(NY)], axis=0) for m in range(3)
        ]
        for m in range(3):
            full = lax.dot_general(tok[m // 2], grads[m], contract_first, preferred_element_type=F32)
            b["wg"][m] = full.reshape(NZ, 2, 2, LANES // 4, n)
        copies = go([remote(b["wg"].at[:, :, :, 1 - c], b["cr"], c_s.at[k], c_r.at[k], sibling)])
        part = jnp.dot(grads[0], b["g"][0], preferred_element_type=F32)
        part = part + jnp.dot(grads[1], b["g"][1], preferred_element_type=F32)
        return copies, part

    def over_y(k, copies):
        arrived(copies)
        b = bufs[k]
        b["ls"][...] = (b["wg"][:, :, 1 - yl, c] + b["cr"][:, :, 1 - yl]).astype(BF16)
        return go([remote(b["ls"], b["lr"], l_s.at[k], l_r.at[k], across)])

    def over_z(k, copies):
        arrived(copies)
        b = bufs[k]
        for m in range(3):
            done = b["wg"][m, :, yl, c] + b["cr"][m, :, yl] + b["lr"][m].astype(F32)
            b["fs"][:, m] = done.astype(BF16)
        b["fr"][z] = b["fs"][z]
        return go([
            remote(b["fs"].at[zj(j)], b["fr"].at[z], z_s.at[k, j], z_r.at[k, j], at_z(zj(j)))
            for j in FAR_FIRST
        ])

    def finish(k, copies):
        arrived(copies)
        b = bufs[k]
        n = CHUNKS[k]
        for m in range(3):
            row = jnp.concatenate([b["fr"][q, m] for q in range(NZ)], axis=1)
            grad_out[m, :, bases[k]:bases[k] + NZ * n] = row

    r0 = project(0)
    forward(1)
    r1 = project(1)
    y0 = activate(0, r0)
    c0, ig0 = backward(0, y0)
    ig_sum[...] = ig0
    y1 = activate(1, r1)
    l0 = over_y(0, c0)
    c1, ig1 = backward(1, y1)
    total = ig_sum[...] + ig1
    ig_sum[...] = total
    for q in range(NX):
        ig_send[q] = total[q * rows_x:(q + 1) * rows_x].astype(BF16)
    ix = go([
        remote(ig_send.at[xj(j)], ig_recv.at[j], ix_s.at[j], ix_r.at[j], at_x(xj(j))) for j in FAR_FIRST
    ])
    z0 = over_z(0, l0)
    l1 = over_y(1, c1)
    finish(0, z0)
    z1 = over_z(1, l1)
    arrived(ix)
    mine = ig_sum[my_rows, :]
    for j in range(1, NX):
        mine = mine + ig_recv[j].astype(F32)
    for q in range(NZ):
        ig_blocks[0, q] = mine[:, q * LANES:(q + 1) * LANES]
    iz = go([
        remote(ig_blocks.at[0, zj(j)], ig_blocks.at[1, j], iz_s.at[j], iz_r.at[j], at_z(zj(j))) for j in FAR_FIRST
    ])
    finish(1, z1)
    arrived(iz)
    result = ig_blocks[0, z]
    for j in range(1, NZ):
        result = result + ig_blocks[1, j]
    ig_out[...] = result
    for cp in pending:
        cp.wait_send()


def widen(ig_in, grad_in, ig_out, gate_out, up_out, down_out):
    ig_out[...] = ig_in[...]
    gate_out[...] = grad_in[0].astype(F32)
    up_out[...] = grad_in[1].astype(F32)
    down_out[...] = grad_in[2].astype(F32)


def local(tokens, cotangent, gate_weight, up_weight, down_weight):
    rows, units_all = tokens.shape[0], gate_weight.shape[0]
    wide = NZ * LANES
    feats = LANES // 4
    scratch = [
        pltpu.VMEM((2, rows, LANES), BF16),
        pltpu.VMEM((3, units_all, LANES), BF16),
        pltpu.VMEM((2, rows, wide), BF16),
        pltpu.VMEM((NX, rows // NX, wide), BF16),
        pltpu.VMEM((NX, rows // NX, wide), BF16),
        pltpu.VMEM((rows, wide), F32),
        pltpu.VMEM((2, NZ, rows // NX, LANES), F32),
    ]
    for n in CHUNKS:
        scratch += [
            pltpu.VMEM((3, n, wide), BF16),
            pltpu.VMEM((NY, 3, rows // NY, n), F32),
            pltpu.VMEM((NY - 1, 3, rows // NY, n), F32),
            pltpu.VMEM((NY, 3, rows // NY, n), BF16),
            pltpu.VMEM((3, NZ, 2, 2, feats, n), F32),
            pltpu.VMEM((3, NZ, 2, feats, n), F32),
            pltpu.VMEM((3, NZ, feats, n), BF16),
            pltpu.VMEM((3, NZ, feats, n), BF16),
            pltpu.VMEM((NZ, 3, feats, n), BF16),
            pltpu.VMEM((NZ, 3, feats, n), BF16),
        ]
    nc = len(CHUNKS)
    dma = pltpu.SemaphoreType.DMA
    scratch += [dma((5,)), dma((NZ,)), dma((NZ,)), dma((2, NX // 2, 4)), dma((2, NX // 2, 4)), dma((1 + nc,))]
    for shape in ((nc, NZ), (nc,), (nc, NY), (nc, NY), (nc,), (nc,), (nc, NZ), (NX,), (NZ,)):
        scratch += [dma(shape), dma(shape)]
    vmem = pl.BlockSpec(memory_space=pltpu.VMEM)
    hbm = pl.BlockSpec(memory_space=pltpu.HBM)
    ig, grads = pl.pallas_call(
        kernel,
        out_shape=(
            jax.ShapeDtypeStruct((rows // NX, LANES), F32),
            jax.ShapeDtypeStruct((3, feats, units_all), BF16),
        ),
        in_specs=[hbm] * 5,
        out_specs=(vmem, vmem),
        scratch_shapes=scratch,
        compiler_params=pltpu.CompilerParams(
            collective_id=0, has_side_effects=True, vmem_limit_bytes=60 * 2**20
        ),
    )(tokens, cotangent, gate_weight, up_weight, down_weight)
    grad = jax.ShapeDtypeStruct((feats, units_all), F32)
    input_grad, *weight_grads = pl.pallas_call(
        widen,
        out_shape=(jax.ShapeDtypeStruct(ig.shape, F32), grad, grad, grad),
    )(ig, grads)
    return (input_grad, *[g.T for g in weight_grads])


def solution(mesh):
    return jax.shard_map(
        local,
        mesh=mesh,
        in_specs=(
            P("dp", "blk"),
            P("dp", "blk"),
            P("hid", "blk"),
            P("hid", "blk"),
            P("hid", "blk"),
        ),
        out_specs=(
            P(("dp", "hid"), "blk"),
            P("hid", ("blk", "dp")),
            P("hid", ("blk", "dp")),
            P("hid", ("blk", "dp")),
        ),
        check_vma=False,
    )
```

```python
import jax
import jax.numpy as jnp
from jax import lax
from jax.experimental import pallas as pl
from jax.experimental.pallas import tpu as pltpu
from jax.sharding import PartitionSpec as P

MESH = pl.DeviceIdType.MESH
NZ, NY, NX = 8, 4, 8
LANES = 128
CHUNKS = (128, 96)
F32, BF16 = jnp.float32, jnp.bfloat16
contract_last = (((1,), (1,)), ((), ()))
contract_first = (((0,), (0,)), ((), ()))
FAR_FIRST = (4, 3, 5, 2, 6, 1, 7)


def kernel(
    tok_in, cot_in, gate_w, up_w, down_w,
    ig_out, grad_out,
    tok_own, w_own, tok, ig_send, ig_recv, ig_send_z, ig_recv_z, ig_sum, ig_blocks, ig_blocks_x,
    *rest,
):
    n_chunks = len(CHUNKS)
    names = ("g", "p", "rp", "h", "wg", "cr", "ls", "lr", "fs", "fr")
    bufs = []
    for k in range(n_chunks):
        bufs.append(dict(zip(names, rest[k * len(names):(k + 1) * len(names)])))
    (
        in_s, tz_s, tz_r, xr_s, xr_r, own_s,
        a_s, a_r, f_s, f_r, r_s, r_r, y_s, y_r, c_s, c_r, l_s, l_r, z_s, z_r,
        ix_s, ix_r, iz_s, iz_r, bz_s, bz_r, bx_s, bx_r,
    ) = rest[n_chunks * len(names):]

    dp = lax.axis_index("dp")
    blk = lax.axis_index("blk")
    x = lax.axis_index("hid")
    yh, z = blk // NZ, blk % NZ
    yl, c = dp // 2, dp % 2
    bases = [NZ * sum(CHUNKS[:k]) for k in range(n_chunks)]

    loads = []
    for i, ref in enumerate((tok_in, cot_in)):
        loads.append(pltpu.make_async_copy(ref, tok_own.at[i], in_s.at[i]))
    for i, ref in enumerate((gate_w, up_w, down_w)):
        loads.append(pltpu.make_async_copy(ref, w_own.at[i], in_s.at[2 + i]))
    for cp in loads:
        cp.start()

    def at_z(v):
        return (dp, yh * NZ + v, x)

    def at_y(v):
        return (dp, v * NZ + z, x)

    def at_x(v):
        return (dp, blk, v)

    sibling = (yl * 2 + 1 - c, blk, x)
    across = ((1 - yl) * 2 + c, blk, x)

    def zj(j):
        return lax.rem(z + j, NZ)

    def yj(j):
        return lax.rem(yh + j, NY)

    def xj(j):
        return lax.rem(x + j, NX)

    barrier = pltpu.get_barrier_semaphore()
    peers = [at_z(zj(j)) for j in range(1, NZ)]
    peers += [at_x(xj(j)) for j in range(1, NX)]
    peers += [at_y(yj(j)) for j in range(1, NY)]
    peers += [sibling, across]
    for p in peers:
        pl.semaphore_signal(barrier, inc=1, device_id=p, device_id_type=MESH)
    pl.semaphore_wait(barrier, len(peers))

    pending = []

    def remote(src, dst, ss, rs, dev):
        return pltpu.make_async_remote_copy(
            src_ref=src, dst_ref=dst, send_sem=ss, recv_sem=rs,
            device_id=dev, device_id_type=MESH,
        )

    def go(copies):
        for cp in copies:
            cp.start()
        pending.extend(copies)
        return copies

    def arrived(copies):
        for cp in copies:
            cp.wait_recv()

    rows_x = tok_in.shape[0] // NX
    my_rows = pl.ds(pl.multiple_of(x * rows_x, rows_x), rows_x)
    my_lanes = pl.ds(pl.multiple_of(z * LANES, LANES), LANES)
    loads[0].wait()
    loads[1].wait()
    tz = go([
        remote(tok_own.at[:, my_rows, :], tok.at[:, my_rows, my_lanes], tz_s.at[j], tz_r.at[j], at_z(zj(j)))
        for j in FAR_FIRST
    ])

    def w_rows(k, to):
        nh = CHUNKS[k] // 2
        return pl.ds(pl.multiple_of(bases[k] + to * CHUNKS[k] + c * nh, 16), nh)

    def half(k, who):
        nh = CHUNKS[k] // 2
        return pl.ds(pl.multiple_of(who * nh, 16), nh)

    def push_weights(k):
        g = bufs[k]["g"]
        return go([
            remote(w_own.at[:, w_rows(k, zj(j)), :], g.at[:, half(k, c), my_lanes], a_s.at[k, j], a_r.at[k, j], at_z(zj(j)))
            for j in FAR_FIRST
        ])

    for cp in loads[2:]:
        cp.wait()
    a_copies = [push_weights(0), push_weights(1)]
    owns = [pltpu.make_async_copy(tok_own.at[:, my_rows, :], tok.at[:, my_rows, my_lanes], own_s.at[0])]
    for k in range(n_chunks):
        owns.append(pltpu.make_async_copy(
            w_own.at[:, w_rows(k, z), :], bufs[k]["g"].at[:, half(k, c), my_lanes], own_s.at[1 + k]))
    for cp in owns:
        cp.start()
    for cp in owns:
        cp.wait()
    arrived(tz)

    f_copies = []

    def forward(k):
        arrived(a_copies[k])
        g = bufs[k]["g"].at[:, half(k, c), :]
        f_copies.append(go([remote(g, g, f_s.at[k], f_r.at[k], sibling)]))

    part = rows_x // 2

    def slice_at(d, i):
        row = lax.rem(x + d + NX, NX) * rows_x + i % 2 * part
        return i // 2, pl.ds(pl.multiple_of(row, part), part)

    moving = {}
    for t in range(1, NX // 2 + 1):
        for i in range(4):
            for way in range(2):
                if t > 1:
                    arrived(moving.pop((t - 1, i, way)))
            for way in range(2):
                if t == NX // 2 and i // 2 != way:
                    continue
                a, where = slice_at(1 - t if way == 0 else t - 1, i)
                ref = tok.at[a, where, :]
                moving[t, i, way] = go([
                    remote(ref, ref, xr_s.at[way, t - 1, i], xr_r.at[way, t - 1, i], at_x(xj(1 if way == 0 else NX - 1)))
                ])
        if t == NX // 2:
            forward(0)
    for copies in moving.values():
        arrived(copies)

    rows_y = tok_in.shape[0] // NY

    def project(k):
        arrived(f_copies[k])
        b = bufs[k]
        for m in range(3):
            part = lax.dot_general(tok[m // 2], b["g"][m], contract_last, preferred_element_type=F32)
            for q in range(NY):
                b["p"][q, m] = part[q * rows_y:(q + 1) * rows_y]
        return go([
            remote(b["p"].at[yj(j)], b["rp"].at[j - 1], r_s.at[k, j], r_r.at[k, j], at_y(yj(j)))
            for j in (2, 1, 3)
        ])

    def activate(k, copies):
        arrived(copies)
        b = bufs[k]
        gate_pre, up_pre, grad_hidden = [
            b["p"][yh, m] + b["rp"][0, m] + b["rp"][1, m] + b["rp"][2, m] for m in range(3)
        ]
        s = jax.nn.sigmoid(gate_pre)
        silu = gate_pre * s
        b["h"][yh, 0] = (grad_hidden * up_pre * s * (1.0 + gate_pre * (1.0 - s))).astype(BF16)
        b["h"][yh, 1] = (grad_hidden * silu).astype(BF16)
        b["h"][yh, 2] = (silu * up_pre).astype(BF16)
        mine = b["h"].at[yh]
        return go([
            remote(mine, mine, y_s.at[k, j], y_r.at[k, j], at_y(yj(j))) for j in (2, 1, 3)
        ])

    def backward(k, copies):
        arrived(copies)
        b = bufs[k]
        n = CHUNKS[k]
        grads = [
            jnp.concatenate([b["h"][q, m] for q in range(NY)], axis=0) for m in range(3)
        ]
        for m in range(3):
            full = lax.dot_general(tok[m // 2], grads[m], contract_first, preferred_element_type=F32)
            b["wg"][m] = full.reshape(NZ, 2, 2, LANES // 4, n)
        copies = go([remote(b["wg"].at[:, :, :, 1 - c], b["cr"], c_s.at[k], c_r.at[k], sibling)])
        part = jnp.dot(grads[0], b["g"][0], preferred_element_type=F32)
        part = part + jnp.dot(grads[1], b["g"][1], preferred_element_type=F32)
        return copies, part

    def over_y(k, copies):
        arrived(copies)
        b = bufs[k]
        b["ls"][...] = (b["wg"][:, :, 1 - yl, c] + b["cr"][:, :, 1 - yl]).astype(BF16)
        return go([remote(b["ls"], b["lr"], l_s.at[k], l_r.at[k], across)])

    def over_z(k, copies):
        arrived(copies)
        b = bufs[k]
        for m in range(3):
            done = b["wg"][m, :, yl, c] + b["cr"][m, :, yl] + b["lr"][m].astype(F32)
            b["fs"][:, m] = done.astype(BF16)
        b["fr"][z] = b["fs"][z]
        return go([
            remote(b["fs"].at[zj(j)], b["fr"].at[z], z_s.at[k, j], z_r.at[k, j], at_z(zj(j)))
            for j in FAR_FIRST
        ])

    def finish(k, copies):
        arrived(copies)
        b = bufs[k]
        n = CHUNKS[k]
        for m in range(3):
            row = jnp.concatenate([b["fr"][q, m] for q in range(NZ)], axis=1)
            grad_out[m, :, bases[k]:bases[k] + NZ * n] = row

    r0 = project(0)
    forward(1)
    r1 = project(1)
    y0 = activate(0, r0)
    c0, ig0 = backward(0, y0)
    ig_sum[...] = ig0
    y1 = activate(1, r1)
    l0 = over_y(0, c0)
    c1, ig1 = backward(1, y1)
    total = ig_sum[...] + ig1
    ig_sum[...] = total
    for q in range(NX):
        rows_q = total[q * rows_x:(q + 1) * rows_x]
        ig_send[q] = rows_q[:part].astype(BF16)
        for w in range(NZ):
            ig_send_z[w, q] = rows_q[part:, w * LANES:(w + 1) * LANES].astype(BF16)
    ix = go([
        remote(ig_send.at[xj(j)], ig_recv.at[j], ix_s.at[j], ix_r.at[j], at_x(xj(j))) for j in FAR_FIRST
    ])
    bz = go([
        remote(ig_send_z.at[zj(j)], ig_recv_z.at[j], bz_s.at[j], bz_r.at[j], at_z(zj(j))) for j in FAR_FIRST
    ])
    z0 = over_z(0, l0)
    l1 = over_y(1, c1)
    finish(0, z0)
    z1 = over_z(1, l1)
    arrived(ix)
    mine = ig_sum[pl.ds(pl.multiple_of(x * rows_x, part), part), :]
    for j in range(1, NX):
        mine = mine + ig_recv[j].astype(F32)
    for q in range(NZ):
        ig_blocks[0, q] = mine[:, q * LANES:(q + 1) * LANES]
    iz = go([
        remote(ig_blocks.at[0, zj(j)], ig_blocks.at[1, j], iz_s.at[j], iz_r.at[j], at_z(zj(j))) for j in FAR_FIRST
    ])
    arrived(bz)
    for q in range(NX):
        block = ig_sum[q * rows_x + part:(q + 1) * rows_x, my_lanes]
        for j in range(1, NZ):
            block = block + ig_recv_z[j, q].astype(F32)
        ig_blocks_x[0, q] = block
    bx = go([
        remote(ig_blocks_x.at[0, xj(j)], ig_blocks_x.at[1, j], bx_s.at[j], bx_r.at[j], at_x(xj(j))) for j in FAR_FIRST
    ])
    finish(1, z1)
    for i, (copies, blocks, own) in enumerate(((iz, ig_blocks, z), (bx, ig_blocks_x, x))):
        arrived(copies)
        result = blocks[0, own]
        for j in range(1, NZ):
            result = result + blocks[1, j]
        ig_out[i * part:(i + 1) * part, :] = result
    for cp in pending:
        cp.wait_send()


def widen(ig_in, grad_in, ig_out, gate_out, up_out, down_out):
    ig_out[...] = ig_in[...]
    gate_out[...] = grad_in[0].astype(F32)
    up_out[...] = grad_in[1].astype(F32)
    down_out[...] = grad_in[2].astype(F32)


def local(tokens, cotangent, gate_weight, up_weight, down_weight):
    rows, units_all = tokens.shape[0], gate_weight.shape[0]
    wide = NZ * LANES
    part = rows // NX // 2
    feats = LANES // 4
    scratch = [
        pltpu.VMEM((2, rows, LANES), BF16),
        pltpu.VMEM((3, units_all, LANES), BF16),
        pltpu.VMEM((2, rows, wide), BF16),
        pltpu.VMEM((NX, part, wide), BF16),
        pltpu.VMEM((NX, part, wide), BF16),
        pltpu.VMEM((NZ, NX, part, LANES), BF16),
        pltpu.VMEM((NZ, NX, part, LANES), BF16),
        pltpu.VMEM((rows, wide), F32),
        pltpu.VMEM((2, NZ, part, LANES), F32),
        pltpu.VMEM((2, NX, part, LANES), F32),
    ]
    for n in CHUNKS:
        scratch += [
            pltpu.VMEM((3, n, wide), BF16),
            pltpu.VMEM((NY, 3, rows // NY, n), F32),
            pltpu.VMEM((NY - 1, 3, rows // NY, n), F32),
            pltpu.VMEM((NY, 3, rows // NY, n), BF16),
            pltpu.VMEM((3, NZ, 2, 2, feats, n), F32),
            pltpu.VMEM((3, NZ, 2, feats, n), F32),
            pltpu.VMEM((3, NZ, feats, n), BF16),
            pltpu.VMEM((3, NZ, feats, n), BF16),
            pltpu.VMEM((NZ, 3, feats, n), BF16),
            pltpu.VMEM((NZ, 3, feats, n), BF16),
        ]
    nc = len(CHUNKS)
    dma = pltpu.SemaphoreType.DMA
    scratch += [dma((5,)), dma((NZ,)), dma((NZ,)), dma((2, NX // 2, 4)), dma((2, NX // 2, 4)), dma((1 + nc,))]
    for shape in ((nc, NZ), (nc,), (nc, NY), (nc, NY), (nc,), (nc,), (nc, NZ), (NX,), (NZ,), (NZ,), (NX,)):
        scratch += [dma(shape), dma(shape)]
    vmem = pl.BlockSpec(memory_space=pltpu.VMEM)
    hbm = pl.BlockSpec(memory_space=pltpu.HBM)
    ig, grads = pl.pallas_call(
        kernel,
        out_shape=(
            jax.ShapeDtypeStruct((rows // NX, LANES), F32),
            jax.ShapeDtypeStruct((3, feats, units_all), BF16),
        ),
        in_specs=[hbm] * 5,
        out_specs=(vmem, vmem),
        scratch_shapes=scratch,
        compiler_params=pltpu.CompilerParams(
            collective_id=0, has_side_effects=True, vmem_limit_bytes=60 * 2**20
        ),
    )(tokens, cotangent, gate_weight, up_weight, down_weight)
    grad = jax.ShapeDtypeStruct((feats, units_all), F32)
    input_grad, *weight_grads = pl.pallas_call(
        widen,
        out_shape=(jax.ShapeDtypeStruct(ig.shape, F32), grad, grad, grad),
    )(ig, grads)
    return (input_grad, *[g.T for g in weight_grads])


def solution(mesh):
    return jax.shard_map(
        local,
        mesh=mesh,
        in_specs=(
            P("dp", "blk"),
            P("dp", "blk"),
            P("hid", "blk"),
            P("hid", "blk"),
            P("hid", "blk"),
        ),
        out_specs=(
            P(("dp", "hid"), "blk"),
            P("hid", ("blk", "dp")),
            P("hid", ("blk", "dp")),
            P("hid", ("blk", "dp")),
        ),
        check_vma=False,
    )
```
